32 devices in a mesh: dom: 8 (over z, y), sub: 4 (over x, core).
Axes of the slice: x: 2, y: 2, z: 4, core: 2. Of those that a mesh axis runs over, the one named last changes fastest.
Arguments:
- charges: float32 [4096, 256], P(('dom', 'sub')), may hold values from -0.3 to 0.3
- points: float32 [3, 4096, 256], P(None, ('dom', 'sub')), may hold values from -1 to 1
- leaf_basis: float32 [4096, 64, 256], P(('dom', 'sub')), may hold values from -0.375 to 0.375
- child_transfer: float32 [4096, 64, 64], P(('dom', 'sub')), may hold values from -0.75 to 0.75
- parent_transfer: float32 [512, 64, 64], P(('dom', 'sub')), may hold values from -0.75 to 0.75
- nodes_leaf: float32 [3, 4096, 64], P(None, ('dom', 'sub')), may hold values from -2 to 2
- nodes_mid: float32 [3, 512, 64], P(None, ('dom', 'sub')), may hold values from -2 to 2
- nodes_top: float32 [3, 64, 64], P(None, ('dom', 'sub')), may hold values from -2 to 2
- near_list: int32 [4096, 6], P(('dom', 'sub')), may hold values from -1 to 4095, as said below
- far_leaf: int32 [4096, 16], P(('dom', 'sub')), may hold values from -1 to 4095, as said below
- far_mid: int32 [512, 16], P(('dom', 'sub')), may hold values from -1 to 511, as said below
- far_top: int32 [64, 16], P(('dom', 'sub')), may hold values from -1 to 63, as said below
Outputs:
- potential: float32 [4096, 256], P(('dom', 'sub'))
The draws below stay inside these ranges and needn't reach their ends.
Inputs may be any that keep to these rules, and one draw needn't show every extreme that they name: `near_list`: -1 marks an empty entry; a row's live entries come first, and its first entry is the leaf itself. Row l names only leaves of the aligned block of 128 leaves that holds l or of the blocks beside it. Some rows have all 6 entries live. `far_leaf`: -1 marks an empty entry; a row's live entries come first. Within each aligned block of 128 rows, the entries, empty ones counted, name clusters of each aligned block of 128 clusters exactly 64 times; in some row blocks all entries are live. `far_mid`: -1 marks an empty entry; a row's live entries come first. Within each aligned block of 16 rows, the entries, empty ones counted, name clusters of each aligned block of 16 clusters exactly 8 times; in some row blocks all entries are live. `far_top`: -1 marks an empty entry; a row's live entries come first; in some aligned blocks of 2 rows all entries are live.
All inputs are finite; a program needn't handle non-finite values.
Results may differ from the reference program's by a relative error of at most 0.0003.
Values sent between devices are 32-bit elements; how exact they have to be, the bound alone decides.
A program may use at most 64 MiB of HBM per device.

```python
import jax
import jax.numpy as jnp
from jax import lax

P_SIZE = 256
R = 64
LEAF_DEV = 128
KN = 6
KF = 16
SHARDS = 32
LEAVES = 4096
CL1 = 512
CL2 = 64


def device_counts(key, shards, rows, most):
    shifted = jax.random.randint(jax.random.fold_in(key, 1), (), 0, 4)
    heavy = (jnp.arange(shards) + shifted) % 4 == 0
    light = jax.random.randint(jax.random.fold_in(key, 2), (shards, rows), 1, most // 2 + 1)
    return jnp.where(heavy[:, None], most, light)


def far_lists(key, rows):
    orders = jax.vmap(lambda sub_key: jax.random.permutation(sub_key, SHARDS))(jax.random.split(jax.random.fold_in(key, 3), SHARDS))
    entries = jnp.arange(rows * KF)
    owners = (jnp.arange(SHARDS)[:, None] + orders[:, entries % SHARDS]) % SHARDS
    wanted = jax.random.randint(jax.random.fold_in(key, 4), (SHARDS, rows * KF), 0, rows)
    cluster_ids = (owners * rows + wanted).reshape(SHARDS, rows, KF)
    counts_live = device_counts(key, SHARDS, rows, KF)
    live = jnp.arange(KF)[None, None, :] < counts_live[:, :, None]
    return jnp.where(live, cluster_ids, -1).reshape(SHARDS * rows, KF).astype(jnp.int32)


def draw_far_leaf(key, part):
    return far_lists(jax.random.fold_in(key, 11), LEAF_DEV)


def draw_far_mid(key, part):
    return far_lists(jax.random.fold_in(key, 12), LEAF_DEV // 8)


def draw_far_top(key, part):
    rows = LEAF_DEV // 64
    base_key = jax.random.fold_in(key, 13)
    cluster_ids = jax.random.randint(jax.random.fold_in(base_key, 5), (SHARDS * rows, KF), 0, CL2)
    counts_live = device_counts(base_key, SHARDS, rows, KF).reshape(-1)
    live = jnp.arange(KF)[None, :] < counts_live[:, None]
    return jnp.where(live, cluster_ids, -1).astype(jnp.int32)


def draw_near_list(key, part):
    base_key = jax.random.fold_in(key, 14)
    leaves_all = jnp.arange(LEAVES)
    blocks = leaves_all // LEAF_DEV
    lower = jnp.maximum(blocks - 1, 0) * LEAF_DEV
    upper = jnp.minimum(blocks + 2, SHARDS) * LEAF_DEV
    raw_draw = jax.random.randint(jax.random.fold_in(base_key, 6), (LEAVES, KN), 0, 3 * LEAF_DEV)
    leaf_ids = lower[:, None] + raw_draw % (upper - lower)[:, None]
    leaf_ids = leaf_ids.at[:, 0].set(leaves_all)
    counts_live = device_counts(base_key, SHARDS, LEAF_DEV, KN).reshape(-1)
    live = jnp.arange(KN)[None, :] < counts_live[:, None]
    return jnp.where(live, leaf_ids, -1).astype(jnp.int32)


def levels(key, extent, cuts, smallest, top_value):
    def one(dim, shards_of):
        heights = jax.random.uniform(jax.random.fold_in(jax.random.fold_in(key, 6), dim), (shards_of,), jnp.float32, smallest / len(cuts), top_value / len(cuts))
        return jnp.repeat(jnp.exp(heights), extent[dim] // shards_of).reshape((-1,) + (1,) * (len(extent) - dim - 1))

    level = one(*cuts[0])
    for cut in cuts[1:]:
        level = level * one(*cut)
    return level


def noise(own_key, dims, scale, reach, cuts=(), dtype=jnp.bfloat16):
    loudness = levels(own_key, dims, cuts, -0.22, 0.18) if cuts else 1.0
    array = jax.random.normal(own_key, dims, jnp.float32) * scale * loudness
    return jnp.minimum(jnp.maximum(array, -reach), reach).astype(dtype)


def setup_inputs(seed: int = 0) -> dict:
    key_list = jax.random.split(jax.random.key(seed), 13)
    return {
        "charges": noise(key_list[0], (LEAVES, P_SIZE), 0.05, 0.3, ((0, 32),), jnp.float32),
        "points": jnp.clip(jax.random.uniform(key_list[1], (3, LEAVES, P_SIZE), jnp.float32, -1.0, 1.0) * levels(key_list[1], (3, LEAVES, P_SIZE), ((1, 32),), -0.4, 0.0), -1.0, 1.0),
        "leaf_basis": noise(key_list[2], (LEAVES, R, P_SIZE), P_SIZE ** -0.5, 0.375, ((0, 32),), jnp.float32),
        "child_transfer": noise(key_list[3], (LEAVES, R, R), R ** -0.5, 0.75, ((0, 32),), jnp.float32),
        "parent_transfer": noise(key_list[4], (CL1, R, R), R ** -0.5, 0.75, ((0, 32),), jnp.float32),
        "nodes_leaf": jnp.clip(jax.random.uniform(key_list[5], (3, LEAVES, R), jnp.float32, -2.0, 2.0) * levels(key_list[5], (3, LEAVES, R), ((1, 32),), -0.4, 0.0), -2.0, 2.0),
        "nodes_mid": jnp.clip(jax.random.uniform(key_list[6], (3, CL1, R), jnp.float32, -2.0, 2.0) * levels(key_list[6], (3, CL1, R), ((1, 32),), -0.4, 0.0), -2.0, 2.0),
        "nodes_top": jnp.clip(jax.random.uniform(key_list[7], (3, CL2, R), jnp.float32, -2.0, 2.0) * levels(key_list[7], (3, CL2, R), ((1, 32),), -0.4, 0.0), -2.0, 2.0),
        "near_list": draw_near_list(jax.random.fold_in(key_list[12], 71), 0),
        "far_leaf": draw_far_leaf(jax.random.fold_in(key_list[12], 71), 0),
        "far_mid": draw_far_mid(jax.random.fold_in(key_list[12], 71), 0),
        "far_top": draw_far_top(jax.random.fold_in(key_list[12], 71), 0),
    }


soften = 0.25
group_rows = 16
block_rows = 32

def kernel(delta_x, delta_y, delta_z):
    return lax.rsqrt(delta_x * delta_x + delta_y * delta_y + delta_z * delta_z + soften)

def near_field(targets, sources, picks_all, validity):
    row_count = targets.shape[1]
    width = targets.shape[2]
    groups = row_count // group_rows
    target_groups = jnp.transpose(targets.reshape(3, groups, group_rows, width), (1, 0, 2, 3))
    pick_groups = picks_all.reshape(groups, group_rows, -1)
    valid_groups = validity.reshape(groups, group_rows, -1).astype(jnp.float32)

    def one_group(pieces):
        target, picks, weights = pieces

        def accumulate(column, running):
            chosen = lax.dynamic_index_in_dim(picks, column, 1, keepdims=False)
            weight = lax.dynamic_index_in_dim(weights, column, 1, keepdims=False)
            nearby = jnp.take(sources, chosen, axis=1)
            values = kernel(target[0][:, :, None] - nearby[0][:, None, :], target[1][:, :, None] - nearby[1][:, None, :], target[2][:, :, None] - nearby[2][:, None, :])
            return running + lax.optimization_barrier(jnp.sum(values * nearby[3][:, None, :], axis=2)) * weight[:, None]
        return lax.fori_loop(0, picks.shape[1], accumulate, jnp.zeros((group_rows, width), jnp.float32))
    return lax.map(one_group, (target_groups, pick_groups, valid_groups)).reshape(row_count, width)

def couple(own_nodes, remote, validity):

    def accumulate(column, running):
        piece = lax.dynamic_index_in_dim(remote, column, 1, keepdims=False)
        weight = lax.dynamic_index_in_dim(validity, column, 1, keepdims=False)
        values = kernel(own_nodes[:, 0, :, None] - piece[:, 1, None, :], own_nodes[:, 1, :, None] - piece[:, 2, None, :], own_nodes[:, 2, :, None] - piece[:, 3, None, :])
        return running + lax.optimization_barrier(jnp.sum(values * piece[:, 0, None, :], axis=2)) * weight[:, None]
    return lax.fori_loop(0, remote.shape[1], accumulate, jnp.zeros((own_nodes.shape[0], own_nodes.shape[2]), jnp.float32))

def make_table(moments, nodes):
    return jnp.concatenate([moments[:, None, :], jnp.transpose(nodes, (1, 0, 2))], axis=1)

def far_level(moments, nodes, lists):
    table = make_table(moments, nodes)
    own_all = jnp.transpose(nodes, (1, 0, 2))
    blocks = lists.shape[0] // block_rows

    def one_block(pieces):
        own_block, list_block = pieces
        validity = (list_block >= 0).astype(jnp.float32)
        remote = jnp.take(table, jnp.maximum(list_block, 0), axis=0)
        return couple(own_block, remote, validity)
    result = lax.map(one_block, (own_all.reshape(blocks, block_rows, 3, -1), lists.reshape(blocks, block_rows, -1)))
    return result.reshape(lists.shape[0], -1)

def reference(charges, points, leaf_basis, child_transfer, parent_transfer, nodes_leaf, nodes_mid, nodes_top, near_list, far_leaf, far_mid, far_top):
    highest = lax.Precision.HIGHEST
    rank_width = leaf_basis.shape[1]
    leaf_moments = jnp.einsum('lrp,lp->lr', leaf_basis, charges, precision=highest)
    mid_moments = jnp.einsum('lij,lj->li', child_transfer, leaf_moments, precision=highest).reshape(-1, 8, rank_width).sum(axis=1)
    top_moments = jnp.einsum('lij,lj->li', parent_transfer, mid_moments, precision=highest).reshape(-1, 8, rank_width).sum(axis=1)
    leaf_local = far_level(leaf_moments, nodes_leaf, far_leaf)
    mid_local = far_level(mid_moments, nodes_mid, far_mid)
    top_local = far_level(top_moments, nodes_top, far_top)
    mid_down = mid_local + jnp.einsum('lji,lj->li', parent_transfer, jnp.repeat(top_local, 8, axis=0), precision=highest)
    leaf_down = leaf_local + jnp.einsum('lji,lj->li', child_transfer, jnp.repeat(mid_down, 8, axis=0), precision=highest)
    sources = jnp.concatenate([points, charges[None]], axis=0)
    near_sum = near_field(points, sources, jnp.maximum(near_list, 0).astype(jnp.int32), near_list >= 0)
    return jnp.einsum('lrp,lr->lp', leaf_basis, leaf_down, precision=highest) + near_sum
```

```python
import functools

import jax
import jax.numpy as jnp
from jax import lax
from jax.experimental import pallas as pl
from jax.experimental.pallas import tpu as pltpu
from jax.sharding import PartitionSpec as P

soften = 0.25
axes = ("dom", "sub")
highest = lax.Precision.HIGHEST


def split(value):
    high = value.astype(jnp.bfloat16).astype(jnp.float32)
    rest = value - high
    middle = rest.astype(jnp.bfloat16).astype(jnp.float32)
    return high, middle, rest - middle


def stack_rows(rows, width):
    place = lax.broadcasted_iota(jnp.int32, (8, width), 0)
    block = jnp.zeros((8, width), jnp.float32)
    for index, row in enumerate(rows):
        block = jnp.where(place == index, row, block)
    return block


def target_side(x, y, z):
    norm = x * x + y * y + z * z + soften
    block = stack_rows((-2.0 * x, -2.0 * y, -2.0 * z, 1.0, norm), x.shape[1])
    high, middle, low = split(block)
    joined = jnp.concatenate([high, high, middle, high, low, middle], axis=0)
    return joined.T.astype(jnp.bfloat16)


def source_side(x, y, z):
    norm = x * x + y * y + z * z
    block = stack_rows((x, y, z, norm, 1.0), x.shape[1])
    high, middle, low = split(block)
    return jnp.concatenate([high, middle, high, low, high, middle], axis=0).astype(jnp.bfloat16)


def near_kernel(entries, first, picks, table, out):
    width = out.shape[1]

    def parts(index):
        row = table[pl.ds(index, 1), :]
        return tuple(row[:, c * width : (c + 1) * width] for c in range(4))

    def one_row(row, carry):
        x, y, z, _ = parts(first + row)
        left = target_side(x, y, z)
        total = jnp.zeros((width, 128), jnp.float32)
        for column in range(entries):
            x, y, z, charge = parts(picks[row * entries + column])
            squares = jnp.dot(left, source_side(x, y, z), preferred_element_type=jnp.float32)
            terms = lax.rsqrt(squares) * charge
            for start in range(0, width, 128):
                total += terms[:, start : start + 128]
        out[pl.ds(row, 1), :] = jnp.sum(total.T, axis=0, keepdims=True)
        return carry

    lax.fori_loop(0, out.shape[0], one_row, 0, unroll=2)


def near_field(picks, table, rows, width, first):
    entries = picks.shape[1]
    return pl.pallas_call(
        functools.partial(near_kernel, entries, first),
        out_shape=jax.ShapeDtypeStruct((rows, width), jnp.float32),
        in_specs=[
            pl.BlockSpec(memory_space=pltpu.SMEM),
            pl.BlockSpec(memory_space=pltpu.VMEM),
        ],
        out_specs=pl.BlockSpec(memory_space=pltpu.VMEM),
        compiler_params=pltpu.CompilerParams(vmem_limit_bytes=32 * 1024 * 1024),
        cost_estimate=pl.CostEstimate(
            flops=rows * entries * width * width * 100,
            bytes_accessed=table.size * 4,
            transcendentals=rows * entries * width * width,
        ),
        name="near",
    )(picks.reshape(-1), table)


def far_kernel(entries, picks, own, table, out):
    rank = out.shape[1]
    lane = lax.broadcasted_iota(jnp.int32, (1, 128), 1)

    def halves(ref, index):
        row = ref[pl.ds(index, 1), :]
        first, second = row[:, :128], row[:, 128:]
        return first, second, pltpu.roll(first, 64, 1), pltpu.roll(second, 64, 1)

    def one_row(row, carry):
        first, second, turned, _ = halves(own, row)
        left = target_side(first, turned, second)[:rank]
        total = jnp.zeros((rank, 128), jnp.float32)
        for pair in range(0, entries, 2):
            a0, a1, a2, a3 = halves(table, picks[row * entries + pair])
            b0, b1, b2, b3 = halves(table, picks[row * entries + pair + 1])
            x = jnp.where(lane < 64, a0, b2)
            y = jnp.where(lane < 64, a2, b0)
            z = jnp.where(lane < 64, a1, b3)
            moment = jnp.where(lane < 64, a3, b1)
            squares = jnp.dot(left, source_side(x, y, z), preferred_element_type=jnp.float32)
            total += lax.rsqrt(squares) * moment
        out[pl.ds(row, 1), :] = jnp.sum(total.T, axis=0, keepdims=True)
        return carry

    lax.fori_loop(0, out.shape[0], one_row, 0, unroll=2)


def far_field(picks, own, table, rows, rank):
    entries = picks.shape[1]
    return pl.pallas_call(
        functools.partial(far_kernel, entries),
        out_shape=jax.ShapeDtypeStruct((rows, rank), jnp.float32),
        in_specs=[
            pl.BlockSpec(memory_space=pltpu.SMEM),
            pl.BlockSpec(memory_space=pltpu.VMEM),
            pl.BlockSpec(memory_space=pltpu.VMEM),
        ],
        out_specs=pl.BlockSpec(memory_space=pltpu.VMEM),
        compiler_params=pltpu.CompilerParams(vmem_limit_bytes=48 * 1024 * 1024),
        cost_estimate=pl.CostEstimate(
            flops=rows * entries * rank * rank * 100,
            bytes_accessed=table.size * 4,
            transcendentals=rows * entries * rank * rank,
        ),
        name="far",
    )(picks.reshape(-1), own, table)


def make_table(moments, nodes):
    return jnp.concatenate([nodes[0], nodes[1], nodes[2], moments], axis=1)


def local(
    charges,
    points,
    leaf_basis,
    child_transfer,
    parent_transfer,
    nodes_leaf,
    nodes_mid,
    nodes_top,
    near_list,
    far_leaf,
    far_mid,
    far_top,
):
    shards = lax.axis_size(axes)
    leaf_count, width = charges.shape
    mid_count = leaf_count // 8
    top_count = mid_count // 8
    rank = leaf_basis.shape[1]

    own_points = jnp.concatenate([points[0], points[1], points[2], charges], axis=1)
    before = lax.ppermute(own_points, axes, [(i, i + 1) for i in range(shards - 1)])
    after = lax.ppermute(own_points, axes, [(i + 1, i) for i in range(shards - 1)])

    leaf_moments = jnp.einsum("lrp,lp->lr", leaf_basis, charges, precision=highest)
    mid_moments = (
        jnp.einsum("lij,lj->li", child_transfer, leaf_moments, precision=highest)
        .reshape(mid_count, 8, rank)
        .sum(axis=1)
    )
    top_moments = (
        jnp.einsum("lij,lj->li", parent_transfer, mid_moments, precision=highest)
        .reshape(top_count, 8, rank)
        .sum(axis=1)
    )
    count = leaf_count + mid_count + top_count
    padded = -(-(count + 1) // 8) * 8
    own = jnp.concatenate(
        [
            make_table(leaf_moments, nodes_leaf),
            make_table(mid_moments, nodes_mid),
            make_table(top_moments, nodes_top),
            jnp.zeros((padded - count, 4 * rank), jnp.float32),
        ],
        axis=0,
    )
    every = lax.all_gather(own, axes, axis=0, tiled=True)

    def rows_of(lists, per_shard, offset):
        row = lists // per_shard * padded + offset + lists % per_shard
        return jnp.where(lists >= 0, row, count)

    far_picks = jnp.concatenate(
        [
            rows_of(far_leaf, leaf_count, 0),
            rows_of(far_mid, mid_count, leaf_count),
            rows_of(far_top, top_count, leaf_count + mid_count),
        ],
        axis=0,
    )

    position = lax.axis_index(axes)
    near_table = jnp.concatenate(
        [before, own_points, after, jnp.zeros((8, 4 * width), jnp.float32)], axis=0
    )
    near_picks = jnp.where(
        near_list >= 0, near_list - (position - 1) * leaf_count, 3 * leaf_count
    )
    near_sum = near_field(near_picks, near_table, leaf_count, width, leaf_count)

    far = far_field(far_picks, own, every, count, rank)
    leaf_local = far[:leaf_count]
    mid_local = far[leaf_count : leaf_count + mid_count]
    top_local = far[leaf_count + mid_count :]
    mid_down = mid_local + jnp.einsum(
        "lji,lj->li", parent_transfer, jnp.repeat(top_local, 8, axis=0), precision=highest
    )
    leaf_down = leaf_local + jnp.einsum(
        "lji,lj->li", child_transfer, jnp.repeat(mid_down, 8, axis=0), precision=highest
    )
    return jnp.einsum("lrp,lr->lp", leaf_basis, leaf_down, precision=highest) + near_sum


def solution(mesh):
    row = P(axes, None)
    plane = P(None, axes, None)
    stack = P(axes, None, None)
    return jax.shard_map(
        local,
        mesh=mesh,
        in_specs=(row, plane, stack, stack, stack, plane, plane, plane, row, row, row, row),
        out_specs=row,
        check_vma=False,
    )
```

```python
import functools

import jax
import jax.numpy as jnp
from jax import lax
from jax.experimental import pallas as pl
from jax.experimental.pallas import tpu as pltpu
from jax.sharding import PartitionSpec as P

soften = 0.25
axes = ("dom", "sub")


def split(value):
    high = value.astype(jnp.bfloat16).astype(jnp.float32)
    rest = value - high
    middle = rest.astype(jnp.bfloat16).astype(jnp.float32)
    return high, middle, rest - middle


def stack_rows(rows, width):
    place = lax.broadcasted_iota(jnp.int32, (8, width), 0)
    block = jnp.zeros((8, width), jnp.float32)
    for index, row in enumerate(rows):
        block = jnp.where(place == index, row, block)
    return block


def target_side(x, y, z):
    norm = x * x + y * y + z * z + soften
    block = stack_rows((-2.0 * x, -2.0 * y, -2.0 * z, 1.0, norm), x.shape[1])
    high, middle, low = split(block)
    joined = jnp.concatenate([high, high, middle, high, low, middle], axis=0)
    return joined.T.astype(jnp.bfloat16)


def source_side(x, y, z):
    norm = x * x + y * y + z * z
    block = stack_rows((x, y, z, norm, 1.0), x.shape[1])
    high, middle, low = split(block)
    return jnp.concatenate([high, middle, high, low, high, middle], axis=0).astype(jnp.bfloat16)


def near_kernel(entries, first, picks, table, out):
    width = out.shape[1]

    def parts(index):
        row = table[pl.ds(index, 1), :]
        return tuple(row[:, c * width : (c + 1) * width] for c in range(4))

    def one_row(row, carry):
        x, y, z, _ = parts(first + row)
        left = target_side(x, y, z)
        total = jnp.zeros((width, 128), jnp.float32)
        for column in range(entries):
            x, y, z, charge = parts(picks[row * entries + column])
            squares = jnp.dot(left, source_side(x, y, z), preferred_element_type=jnp.float32)
            terms = lax.rsqrt(squares) * charge
            for start in range(0, width, 128):
                total += terms[:, start : start + 128]
        out[pl.ds(row, 1), :] = jnp.sum(total.T, axis=0, keepdims=True)
        return carry

    lax.fori_loop(0, out.shape[0], one_row, 0, unroll=8)


def near_field(picks, table, rows, width, first):
    entries = picks.shape[1]
    return pl.pallas_call(
        functools.partial(near_kernel, entries, first),
        out_shape=jax.ShapeDtypeStruct((rows, width), jnp.float32),
        in_specs=[
            pl.BlockSpec(memory_space=pltpu.SMEM),
            pl.BlockSpec(memory_space=pltpu.VMEM),
        ],
        out_specs=pl.BlockSpec(memory_space=pltpu.VMEM),
        compiler_params=pltpu.CompilerParams(vmem_limit_bytes=32 * 1024 * 1024),
        cost_estimate=pl.CostEstimate(
            flops=rows * entries * width * width * 100,
            bytes_accessed=table.size * 4,
            transcendentals=rows * entries * width * width,
        ),
        name="near",
    )(picks.reshape(-1), table)


def far_kernel(entries, picks, own_xy, own_zm, table_xy, table_zm, out, near_xy, near_zm):
    rank = out.shape[1]
    half = entries // 2
    lower = lax.broadcasted_iota(jnp.int32, (half, 128), 1) < 64
    slot = lax.rem(lax.broadcasted_iota(jnp.int32, (rank, 15 * half), 1), half)

    def spread(row):
        return jnp.broadcast_to(row, (half, 128))

    def one_row(row, buffer):
        for e in range(entries):
            pick = picks[row * entries + e]
            near_xy[buffer, pl.ds(e, 1), :] = table_xy[pl.ds(pick, 1), :]
            near_zm[buffer, pl.ds(e, 1), :] = table_zm[pl.ds(pick, 1), :]
        xy = spread(own_xy[pl.ds(row, 1), :])
        zm = spread(own_zm[pl.ds(row, 1), :])
        yx = pltpu.roll(xy, 64, 1)
        ones = jnp.ones((half, 128), jnp.float32)
        left = []
        for value in (xy, yx, zm):
            h, m, _ = split(-2.0 * value)
            left += [h, h, m]
        left += list(split(xy * xy + yx * yx + zm * zm + soften)) + [ones, ones, ones]
        left = jnp.concatenate(left, axis=0)[:, :rank].T
        a, b = near_xy[buffer, :half, :], near_xy[buffer, half:, :]
        c, d = near_zm[buffer, :half, :], near_zm[buffer, half:, :]
        x = jnp.where(lower, a, pltpu.roll(b, 64, 1))
        y = jnp.where(lower, pltpu.roll(a, 64, 1), b)
        z = jnp.where(lower, c, pltpu.roll(d, 64, 1))
        moment = jnp.where(lower, pltpu.roll(c, 64, 1), d)
        right = []
        for value in (x, y, z):
            h, m, _ = split(value)
            right += [h, m, h]
        right += [ones, ones, ones] + list(split(x * x + y * y + z * z))
        right = jnp.concatenate(right, axis=0).astype(jnp.bfloat16)
        total = jnp.zeros((rank, 128), jnp.float32)
        chosen = jnp.concatenate([jnp.where(slot == e, left, 0.0) for e in range(half)], axis=0)
        squares = jnp.dot(
            chosen.astype(jnp.bfloat16), right, preferred_element_type=jnp.float32
        )
        for e in range(half):
            total += lax.rsqrt(squares[e * rank : (e + 1) * rank]) * moment[e : e + 1, :]
        out[pl.ds(row, 1), :] = jnp.sum(total.T, axis=0, keepdims=True)

    unroll = near_xy.shape[0]

    def some_rows(step, carry):
        for buffer in range(unroll):
            one_row(step * unroll + buffer, buffer)
        return carry

    lax.fori_loop(0, out.shape[0] // unroll, some_rows, 0)


def far_field(picks, own_xy, own_zm, table_xy, table_zm, rank):
    rows, entries = picks.shape
    return pl.pallas_call(
        functools.partial(far_kernel, entries),
        out_shape=jax.ShapeDtypeStruct((rows, rank), jnp.float32),
        in_specs=[pl.BlockSpec(memory_space=pltpu.SMEM)]
        + [pl.BlockSpec(memory_space=pltpu.VMEM)] * 4,
        out_specs=pl.BlockSpec(memory_space=pltpu.VMEM),
        scratch_shapes=[pltpu.VMEM((8, entries, 128), jnp.float32)] * 2,
        compiler_params=pltpu.CompilerParams(vmem_limit_bytes=48 * 1024 * 1024),
        cost_estimate=pl.CostEstimate(
            flops=rows * entries * rank * rank * 100,
            bytes_accessed=table_xy.size * 8,
            transcendentals=rows * entries * rank * rank,
        ),
        name="far",
    )(picks.reshape(-1), own_xy, own_zm, table_xy, table_zm)


def contract_last(matrices, vectors):
    return jnp.sum(matrices * vectors[:, None, :], axis=2)


def contract_first(matrices, vectors):
    return jnp.sum(matrices * vectors[:, :, None], axis=1)


def local(
    charges,
    points,
    leaf_basis,
    child_transfer,
    parent_transfer,
    nodes_leaf,
    nodes_mid,
    nodes_top,
    near_list,
    far_leaf,
    far_mid,
    far_top,
):
    shards = lax.axis_size(axes)
    leaf_count, width = charges.shape
    mid_count = leaf_count // 8
    top_count = mid_count // 8
    rank = leaf_basis.shape[1]

    count = leaf_count + mid_count + top_count
    padded = -(-(count + 1) // 8) * 8
    filler = jnp.zeros((padded - count, 2 * rank), jnp.float32)
    nodes = (nodes_leaf, nodes_mid, nodes_top)

    def joined(first, second):
        return jnp.concatenate(
            [jnp.concatenate(pair, axis=1) for pair in zip(first, second)] + [filler], axis=0
        )

    own_xy = joined([n[0] for n in nodes], [n[1] for n in nodes])
    every_xy = lax.all_gather(own_xy, axes, axis=0, tiled=True)

    own_points = jnp.concatenate([points[0], points[1], points[2], charges], axis=1)
    before = lax.ppermute(own_points, axes, [(i, i + 1) for i in range(shards - 1)])
    after = lax.ppermute(own_points, axes, [(i + 1, i) for i in range(shards - 1)])

    leaf_moments = contract_last(leaf_basis, charges)
    mid_moments = (
        contract_last(child_transfer, leaf_moments)
        .reshape(mid_count, 8, rank)
        .sum(axis=1)
    )
    top_moments = (
        contract_last(parent_transfer, mid_moments)
        .reshape(top_count, 8, rank)
        .sum(axis=1)
    )
    own_zm = joined([n[2] for n in nodes], (leaf_moments, mid_moments, top_moments))
    every_zm = lax.all_gather(own_zm, axes, axis=0, tiled=True)

    def rows_of(lists, per_shard, offset):
        row = lists // per_shard * padded + offset + lists % per_shard
        return jnp.where(lists >= 0, row, count)

    far_picks = jnp.concatenate(
        [
            rows_of(far_leaf, leaf_count, 0),
            rows_of(far_mid, mid_count, leaf_count),
            rows_of(far_top, top_count, leaf_count + mid_count),
            jnp.full((padded - count, far_leaf.shape[1]), count, jnp.int32),
        ],
        axis=0,
    )

    position = lax.axis_index(axes)
    near_table = jnp.concatenate(
        [before, own_points, after, jnp.zeros((8, 4 * width), jnp.float32)], axis=0
    )
    near_picks = jnp.where(
        near_list >= 0, near_list - (position - 1) * leaf_count, 3 * leaf_count
    )
    near_sum = near_field(near_picks, near_table, leaf_count, width, leaf_count)

    far = far_field(far_picks, own_xy, own_zm, every_xy, every_zm, rank)
    leaf_local = far[:leaf_count]
    mid_local = far[leaf_count : leaf_count + mid_count]
    top_local = far[leaf_count + mid_count : count]
    mid_down = mid_local + contract_first(parent_transfer, jnp.repeat(top_local, 8, axis=0))
    leaf_down = leaf_local + contract_first(child_transfer, jnp.repeat(mid_down, 8, axis=0))
    return contract_first(leaf_basis, leaf_down) + near_sum


def solution(mesh):
    row = P(axes, None)
    plane = P(None, axes, None)
    stack = P(axes, None, None)
    return jax.shard_map(
        local,
        mesh=mesh,
        in_specs=(row, plane, stack, stack, stack, plane, plane, plane, row, row, row, row),
        out_specs=row,
        check_vma=False,
    )
```
